256 devices in a mesh: ep: 64 (over z, x, core), tp: 4 (over y).
Axes of the slice: x: 4, y: 4, z: 8, core: 2. Of those that a mesh axis runs over, the one named last changes fastest.
Arguments:
- tokens: bfloat16 [1024, 7168], P(('ep', 'tp')), may hold values from -6 to 6
- expert_ids: int32 [1024, 8], P(('ep', 'tp')), may hold values from 0 to 31, all different within a row; in each aligned block of 4 rows (0 to 3, 4 to 7, ...) at most 2 rows name the same one
- affinity: float32 [1024, 8], P(('ep', 'tp')), may hold values from 0.1 to 1
- gate_weight: bfloat16 [64, 7168, 1024], P('ep', None, 'tp'), may hold values from -0.0625 to 0.0625
- up_weight: bfloat16 [64, 7168, 1024], P('ep', None, 'tp'), may hold values from -0.0625 to 0.0625
- down_weight: bfloat16 [64, 1024, 7168], P('ep', 'tp'), may hold values from -0.125 to 0.125
Outputs:
- mixed: bfloat16 [1024, 7168], P(('ep', 'tp'))
The draws below stay inside these ranges and needn't reach their ends.
Inputs may be any that keep to these rules, and one draw needn't show every extreme that they name: `expert_ids`: each row names 8 different experts. Among the 4 rows of one device no expert is named by more than 2 rows, and some device's rows name one expert exactly 2 times.
All inputs are finite; a program needn't handle non-finite values.
Results may differ from the reference program's by a relative error of at most 0.0065.
Values may be sent and summed in bfloat16 or wider, within the bound.
No kernel may reach another device: no remote copies, remote signals or barrier semaphores. Data moves between devices by JAX's collectives and lax.ppermute only.
A program may use at most 128 MiB of HBM per device.

```python
import math
import jax
import jax.numpy as jnp
import numpy as np
from jax import lax

D = 7168
FF = 2048
TOK_DEV = 4
EXPERTS = 32
TOP = 8
MOST = 2
TOKENS = 1024


def block_scale(stream_key, extent, split, low, top_value):
    level, own = 1.0, jax.random.fold_in(stream_key, 6)
    for dim, shards_of in split:
        steps = jnp.exp(jax.random.uniform(jax.random.fold_in(own, dim), (shards_of,), jnp.float32, low / len(split), top_value / len(split)))
        level = level * jnp.repeat(steps, extent[dim] // shards_of).reshape([-1 if axis == dim else 1 for axis in range(len(extent))])
    return level


def assign_block(stream_key, own, number, rows, number_of, top, most, skew):
    ranking = jax.random.permutation(stream_key, number_of)
    heavy_load, usual = shares(number_of, rows * top, most, skew, True), shares(number_of, rows * top, most, skew, False)
    places = jnp.arange(number_of)

    def named(sizes, turn):
        used = int((sizes > 0).sum())
        fixed = max(1, used // 4)
        passed = fixed + (places - fixed + turn * (used - fixed)) % max(1, number_of - fixed)
        return jnp.zeros((number_of,), jnp.int32).at[ranking[jnp.where(places < fixed, places, passed)]].set(jnp.asarray(sizes, jnp.int32))

    sizes = jnp.where(number % 4 == 0, named(heavy_load, number // 4), named(usual, number - number // 4 - 1))
    mixed = jax.random.permutation(jax.random.fold_in(own, 3), number_of)
    source_of, taker = mixed[0:number_of // 2 * 2:2], mixed[1:number_of // 2 * 2:2]
    slack = jnp.minimum(sizes[source_of] - 1, most - sizes[taker]) // 2
    slack = jnp.where((source_of == ranking[0]) | (taker == ranking[0]) | (sizes[taker] == 0), 0, jnp.maximum(slack, 0))
    passed = jax.random.randint(jax.random.fold_in(own, 4), (number_of // 2,), 0, 1 << 20) % (slack + 1)
    sizes = sizes.at[source_of].add(-passed).at[taker].add(passed)
    items = jnp.searchsorted(jnp.cumsum(sizes), jnp.arange(rows * top), side="right").astype(jnp.int32)
    grid = items.reshape(top, rows).T
    grid = grid[jax.random.permutation(jax.random.fold_in(own, 1), rows)]
    turn = jax.random.randint(jax.random.fold_in(own, 2), (rows, 1), 0, top)
    return jnp.take_along_axis(grid, (jnp.arange(top)[None, :] + turn) % top, axis=1)


def shares(count, total, most, skew, full):
    portions = [(1 << 20) // math.isqrt(grade ** skew) + 1 for grade in range(1, count + 1)]
    largest = most if full else min(most, max(-(-total // count), total * portions[0] // sum(portions)))
    least = 1 if total - largest >= count - 1 else 0
    given, surplus = [largest] + [least] * (count - 1), total - largest - least * (count - 1)
    while surplus > 0:
        free = [i for i in range(1, count) if given[i] < largest] or [i for i in range(1, count) if given[i] < most]
        whole, budget = sum([portions[i] for i in free]), surplus
        for i in free:
            extra = min(most - given[i], max(1, budget * portions[i] // whole), surplus)
            given[i] = given[i] + extra
            surplus = surplus - extra
    return np.array(given)


def normal_values(key, dims, spread, limit, shards=(), kind=jnp.bfloat16):
    entries = spread * jax.random.normal(key, dims, jnp.float32)
    if shards:
        entries = entries * block_scale(key, dims, shards, -0.22, 0.18)
    return jnp.clip(entries, -limit, limit).astype(kind)


def setup_inputs(seed: int = 0) -> dict:
    arg_keys = jax.random.split(jax.random.key(seed), 7)
    tokens = normal_values(arg_keys[0], (TOKENS, D), 1.0, 6.0, ((0, 256),))
    expert_ids_keys = jax.random.split(jax.random.fold_in(arg_keys[1], 1), TOKENS // TOK_DEV)
    expert_ids_turns = jax.random.permutation(jax.random.fold_in(arg_keys[1], 3), TOKENS // TOK_DEV)
    expert_ids = jax.vmap(lambda own, number: assign_block(jax.random.fold_in(arg_keys[1], 2), own, number, TOK_DEV, EXPERTS, TOP, MOST, 2))(expert_ids_keys, expert_ids_turns).reshape((TOKENS, TOP))
    affinity = jnp.clip(0.1 + 0.9 * jax.random.uniform(arg_keys[2], (TOKENS, TOP), jnp.float32) ** block_scale(arg_keys[2], (TOKENS, TOP), ((0, 256),), -0.2, 0.2), 0.1, 1.0)
    gate_weight = normal_values(arg_keys[3], (2 * EXPERTS, D, FF // 2), D ** -0.5, 0.0625, ((0, 64), (2, 4)))
    up_weight = normal_values(arg_keys[4], (2 * EXPERTS, D, FF // 2), D ** -0.5, 0.0625, ((0, 64), (2, 4)))
    down_weight = normal_values(arg_keys[5], (2 * EXPERTS, FF // 2, D), FF ** -0.5, 0.125, ((0, 64), (1, 4)))
    return dict(tokens=tokens, expert_ids=expert_ids, affinity=affinity, gate_weight=gate_weight, up_weight=up_weight, down_weight=down_weight)


def reference(tokens, expert_ids, affinity, gate_weight, up_weight, down_weight):
    weights = 2.5 * affinity / jnp.sum(affinity, axis=1, keepdims=True)
    experts = gate_weight.shape[0] // 2

    def half_output(half_index):
        gate_value = jnp.dot(tokens, gate_weight[half_index], preferred_element_type=jnp.float32)
        up_value = jnp.dot(tokens, up_weight[half_index], preferred_element_type=jnp.float32)
        hidden = (jax.nn.silu(gate_value) * up_value).astype(jnp.bfloat16)
        return jnp.dot(hidden, down_weight[half_index], preferred_element_type=jnp.float32).astype(jnp.bfloat16)

    def add_expert(running, expert):
        paired = half_output(2 * expert).astype(jnp.float32) + half_output(2 * expert + 1).astype(jnp.float32)
        expert_output = lax.optimization_barrier(paired.astype(jnp.bfloat16)).astype(jnp.float32)
        weighting = jnp.sum(jnp.where(expert_ids == expert, weights, jnp.float32(0.0)), axis=1)
        return running + weighting[:, None] * expert_output, None

    start_sum = jnp.zeros(tokens.shape, jnp.float32)
    running, _ = lax.scan(add_expert, start_sum, jnp.arange(experts, dtype=jnp.int32))
    return running.astype(jnp.bfloat16)
```

```python
import functools

import jax
import jax.numpy as jnp
from jax import lax
from jax.experimental import pallas as pl
from jax.experimental.pallas import tpu as pltpu
from jax.sharding import PartitionSpec as P

MIB = 1024 * 1024
WAIT = 256 * MIB
PART = 32
ANYWHERE = pl.BlockSpec(memory_space=pl.ANY)
ONCHIP = pl.BlockSpec(memory_space=pltpu.VMEM)


def after(values, *first, cost=0):
    return pl.pallas_call(
        lambda *refs: None,
        in_specs=[ANYWHERE] * (len(values) + len(first)),
        out_specs=[ANYWHERE] * len(values),
        out_shape=[jax.ShapeDtypeStruct(value.shape, value.dtype) for value in values],
        input_output_aliases={place: place for place in range(len(values))},
        compiler_params=pltpu.CompilerParams(vmem_limit_bytes=MIB),
        cost_estimate=pl.CostEstimate(flops=0, bytes_accessed=cost, transcendentals=0),
    )(*values, *first)


def stage_kernel(*refs):
    half = len(refs) // 3
    copies = [
        pltpu.make_async_copy(refs[place], refs[half + place], refs[2 * half + place])
        for place in range(half)
    ]
    for copy in copies:
        copy.start()
    for copy in copies:
        copy.wait()


def stage(*weights):
    return pl.pallas_call(
        stage_kernel,
        in_specs=[pl.BlockSpec(memory_space=pltpu.HBM)] * len(weights),
        out_specs=[ONCHIP] * len(weights),
        out_shape=[pltpu.VMEM(weight.shape, weight.dtype) for weight in weights],
        scratch_shapes=[pltpu.SemaphoreType.DMA] * len(weights),
        compiler_params=pltpu.CompilerParams(vmem_limit_bytes=MIB),
    )(*weights)


def ffn_kernel(pieces, tiles, *refs):
    own_refs, refs = refs[:pieces], refs[pieces:]
    other_refs, refs = refs[:pieces], refs[pieces:]
    gate_ref, up_ref, down_ref, keep_ref, *send_refs = refs
    half, width = keep_ref.shape
    part = half // len(send_refs)
    rows = jnp.concatenate([ref[...] for ref in (*own_refs, *other_refs)], axis=0)
    gate_value = jnp.dot(rows, gate_ref[0], preferred_element_type=jnp.float32)
    up_value = jnp.dot(rows, up_ref[0], preferred_element_type=jnp.float32)
    hidden = gate_value / (1.0 + jnp.exp(-gate_value)) * up_value
    hidden = hidden.astype(jnp.bfloat16)
    for tile in range(tiles):
        span = slice(tile * (width // tiles), (tile + 1) * (width // tiles))
        out = jnp.dot(hidden, down_ref[0, :, span], preferred_element_type=jnp.float32)
        keep_ref[:, span] = out[:half].astype(jnp.bfloat16)
        for place, send_ref in enumerate(send_refs):
            first = half + place * part
            send_ref[:, span] = out[first : first + part].astype(jnp.bfloat16)


def ffn(own, other, gate_weight, up_weight, down_weight):
    half = sum(piece.shape[0] for piece in own)
    width = own[0].shape[1]
    units = gate_weight.shape[2]
    parts = half // PART
    return pl.pallas_call(
        functools.partial(ffn_kernel, len(own), 4),
        in_specs=[ONCHIP] * (2 * len(own) + 3),
        out_specs=[ONCHIP] * (1 + parts),
        out_shape=[jax.ShapeDtypeStruct((half, width), jnp.bfloat16)]
        + [jax.ShapeDtypeStruct((PART, width), jnp.bfloat16)] * parts,
        compiler_params=pltpu.CompilerParams(vmem_limit_bytes=16 * MIB),
        cost_estimate=pl.CostEstimate(
            flops=2 * 2 * half * 3 * width * units,
            bytes_accessed=3 * width * units * 2 + half * width * 8,
            transcendentals=2 * half * units,
        ),
    )(*own, *other, gate_weight, up_weight, down_weight)


def shards(tokens, expert_ids, affinity, gate_weight, up_weight, down_weight):
    ep_count = lax.axis_size("ep")
    tp_count = lax.axis_size("tp")
    experts = ep_count // 2
    tok_count, width = tokens.shape
    top_count = expert_ids.shape[1]
    slots = 2 * max(1, tok_count * top_count // experts)
    count = experts * slots
    half = count // 2
    same_core = [[i for i in range(ep_count) if i % 2 == c] for c in range(2)]

    def over_core(value):
        return lax.ppermute(value, "ep", [(i, i ^ 1) for i in range(ep_count)])

    def over_y(value, shift):
        return lax.ppermute(
            value, "tp", [(i, (i + shift) % tp_count) for i in range(tp_count)]
        )

    def exchange(value):
        return lax.all_to_all(
            value, "ep", split_axis=0, concat_axis=0, axis_index_groups=same_core, tiled=True
        )

    def wide(value):
        return value.astype(jnp.float32)

    def narrow(value):
        return value.astype(jnp.bfloat16)

    weights = 2.5 * affinity / jnp.sum(affinity, axis=1, keepdims=True)
    labels = jnp.arange(experts, dtype=jnp.int32)
    matches = (expert_ids[:, :, None] == labels[None, None, :]).astype(jnp.float32)
    chosen = jnp.sum(matches, axis=1)
    shares = jnp.sum(matches * weights[:, :, None], axis=1)
    earlier = jnp.cumsum(chosen, axis=0) - chosen
    slot_values = jnp.arange(slots, dtype=jnp.float32)
    picked = chosen.T[:, None, :] * (earlier.T[:, None, :] == slot_values[None, :, None]).astype(
        jnp.float32
    )
    picked = picked.reshape(count, tok_count)
    coefficients = picked * jnp.repeat(shares.T, slots, axis=0)
    outgoing = narrow(
        jnp.dot(picked.astype(jnp.bfloat16), tokens, preferred_element_type=jnp.float32)
    )

    staged = stage(gate_weight, up_weight, down_weight)

    own = exchange(outgoing)
    left, right = over_y(own, 1), over_y(own, -1)
    own_kept, *own_sent = ffn([own], [over_core(own)], *staged)
    left, right = after([left, right], own_kept)

    far = [over_y(left[:half], 1), over_y(right[half:], -1)]
    near = [left, right]
    near_kept, *near_sent = ffn(near, [over_core(piece) for piece in near], *staged)
    far = after(far, near_kept, cost=WAIT)
    *near_got, far_low = after([*map(over_core, near_sent), far[0]], far[1])
    far = [far_low, far[1]]
    near_sum = [
        wide(near_kept[place * half : (place + 1) * half]) + wide(got)
        for place, got in enumerate(near_got)
    ]

    to_left, to_right = over_y(narrow(near_sum[0]), -1), over_y(narrow(near_sum[3]), 1)
    far_kept, *far_sent = ffn(far, [over_core(piece) for piece in far], *staged)
    to_left, to_right = after([to_left, to_right], far_kept, cost=WAIT)
    far_got = after([*map(over_core, far_sent)], to_left, to_right)

    passed_right = over_y(narrow(wide(far_kept[:half]) + wide(far_got[0])), 1)
    passed_left = over_y(narrow(wide(far_kept[half:]) + wide(far_got[1])), -1)
    last_right = over_y(narrow(near_sum[2] + wide(passed_right)), 1)
    last_left = over_y(narrow(near_sum[1] + wide(passed_left)), -1)
    own_got = jnp.concatenate([over_core(piece) for piece in own_sent], axis=0)
    from_left = wide(jnp.concatenate([last_right, to_right], axis=0))
    from_right = wide(jnp.concatenate([to_left, last_left], axis=0))
    own_total = wide(own_kept) + wide(own_got)
    returned = exchange(narrow(own_total + from_left + from_right))
    mixed = jnp.dot(
        coefficients.T,
        wide(returned),
        precision=lax.Precision.HIGHEST,
        preferred_element_type=jnp.float32,
    )
    return narrow(mixed)


def solution(mesh):
    return jax.shard_map(
        shards,
        mesh=mesh,
        in_specs=(
            P(("ep", "tp"), None),
            P(("ep", "tp"), None),
            P(("ep", "tp"), None),
            P("ep", None, "tp"),
            P("ep", None, "tp"),
            P("ep", "tp", None),
        ),
        out_specs=P(("ep", "tp"), None),
        check_vma=False,
    )
```

```python
import functools

import jax
import jax.numpy as jnp
from jax import lax
from jax.experimental import pallas as pl
from jax.experimental.pallas import tpu as pltpu
from jax.sharding import PartitionSpec as P

MIB = 1024 * 1024
WAIT = 256 * MIB
PART = 32
ANYWHERE = pl.BlockSpec(memory_space=pl.ANY)
ONCHIP = pl.BlockSpec(memory_space=pltpu.VMEM)


def after(values, *first, cost=0):
    return pl.pallas_call(
        lambda *refs: None,
        in_specs=[ANYWHERE] * (len(values) + len(first)),
        out_specs=[ANYWHERE] * len(values),
        out_shape=[jax.ShapeDtypeStruct(value.shape, value.dtype) for value in values],
        input_output_aliases={place: place for place in range(len(values))},
        compiler_params=pltpu.CompilerParams(vmem_limit_bytes=MIB),
        cost_estimate=pl.CostEstimate(flops=cost * 64, bytes_accessed=cost, transcendentals=0),
    )(*values, *first)


def stage_kernel(*refs):
    half = len(refs) // 3
    copies = [
        pltpu.make_async_copy(refs[place], refs[half + place], refs[2 * half + place])
        for place in range(half)
    ]
    for copy in copies:
        copy.start()
    for copy in copies:
        copy.wait()


def stage(*weights):
    return pl.pallas_call(
        stage_kernel,
        in_specs=[pl.BlockSpec(memory_space=pltpu.HBM)] * len(weights),
        out_specs=[ONCHIP] * len(weights),
        out_shape=[pltpu.VMEM(weight.shape, weight.dtype) for weight in weights],
        scratch_shapes=[pltpu.SemaphoreType.DMA] * len(weights),
        compiler_params=pltpu.CompilerParams(vmem_limit_bytes=MIB),
    )(*weights)


def ffn_kernel(own_count, other_count, tiles, *refs):
    own_refs, refs = refs[:own_count], refs[own_count:]
    other_refs, refs = refs[:other_count], refs[other_count:]
    gate_ref, up_ref, down_ref, keep_ref, *send_refs = refs
    half, width = keep_ref.shape
    part = half // len(send_refs)
    rows = jnp.concatenate([ref[...] for ref in (*own_refs, *other_refs)], axis=0)
    gate_value = jnp.dot(rows, gate_ref[0], preferred_element_type=jnp.float32)
    up_value = jnp.dot(rows, up_ref[0], preferred_element_type=jnp.float32)
    hidden = gate_value / (1.0 + jnp.exp(-gate_value)) * up_value
    hidden = hidden.astype(jnp.bfloat16)
    for tile in range(tiles):
        span = slice(tile * (width // tiles), (tile + 1) * (width // tiles))
        out = jnp.dot(hidden, down_ref[0, :, span], preferred_element_type=jnp.float32)
        keep_ref[:, span] = out[:half].astype(jnp.bfloat16)
        for place, send_ref in enumerate(send_refs):
            first = half + place * part
            send_ref[:, span] = out[first : first + part].astype(jnp.bfloat16)


def ffn(own, other, gate_weight, up_weight, down_weight):
    half = sum(piece.shape[0] for piece in own)
    width = own[0].shape[1]
    units = gate_weight.shape[2]
    parts = half // PART
    return pl.pallas_call(
        functools.partial(ffn_kernel, len(own), len(other), 4),
        in_specs=[ONCHIP] * (len(own) + len(other) + 3),
        out_specs=[ONCHIP] * (1 + parts),
        out_shape=[jax.ShapeDtypeStruct((half, width), jnp.bfloat16)]
        + [jax.ShapeDtypeStruct((PART, width), jnp.bfloat16)] * parts,
        compiler_params=pltpu.CompilerParams(vmem_limit_bytes=16 * MIB),
        cost_estimate=pl.CostEstimate(flops=0, bytes_accessed=0, transcendentals=0),
    )(*own, *other, gate_weight, up_weight, down_weight)


def shards(tokens, expert_ids, affinity, gate_weight, up_weight, down_weight):
    ep_count = lax.axis_size("ep")
    tp_count = lax.axis_size("tp")
    experts = ep_count // 2
    tok_count, width = tokens.shape
    top_count = expert_ids.shape[1]
    slots = 2 * max(1, tok_count * top_count // experts)
    count = experts * slots
    half = count // 2
    same_core = [[i for i in range(ep_count) if i % 2 == c] for c in range(2)]

    def over_core(value):
        return lax.ppermute(value, "ep", [(i, i ^ 1) for i in range(ep_count)])

    def over_y(value, shift):
        return lax.ppermute(
            value, "tp", [(i, (i + shift) % tp_count) for i in range(tp_count)]
        )

    def exchange(value):
        return lax.all_to_all(
            value, "ep", split_axis=0, concat_axis=0, axis_index_groups=same_core, tiled=True
        )

    def wide(value):
        return value.astype(jnp.float32)

    def narrow(value):
        return value.astype(jnp.bfloat16)

    labels = jnp.arange(experts, dtype=jnp.int32)
    matches = (expert_ids[:, :, None] == labels[None, None, :]).astype(jnp.float32)
    chosen = jnp.sum(matches, axis=1)
    earlier = jnp.cumsum(chosen, axis=0) - chosen
    slot_values = jnp.arange(slots, dtype=jnp.float32)
    picked = chosen.T[:, None, :] * (earlier.T[:, None, :] == slot_values[None, :, None]).astype(
        jnp.float32
    )
    picked = picked.reshape(count, tok_count)
    outgoing = narrow(
        jnp.dot(picked.astype(jnp.bfloat16), tokens, preferred_element_type=jnp.float32)
    )

    staged = stage(gate_weight, up_weight, down_weight)

    own = exchange(outgoing)
    low, high = own[:half], own[half:]
    others = [over_core(low), over_core(high)]
    near = [over_y(low, 1), over_y(high, -1)]
    own_kept, *own_sent = ffn([low, high], others, *staged)
    near = [*after(near, own_kept), over_y(high, 1), over_y(low, -1)]

    far = [over_y(near[0], 1), over_y(near[1], -1)]
    quarter = half // 2
    traded = [over_core(part) for piece in near for part in (piece[:quarter], piece[quarter:])]
    near_kept, *near_sent = ffn(near, traded, *staged)
    far = after(far, near_kept, cost=WAIT)
    *near_got, far_low = after([*map(over_core, near_sent), far[0]], far[1])
    far = [far_low, far[1]]
    near_sum = [
        wide(near_kept[place * half : (place + 1) * half]) + wide(got)
        for place, got in enumerate(near_got)
    ]

    to_left, to_right = over_y(narrow(near_sum[0]), -1), over_y(narrow(near_sum[1]), 1)
    far_kept, *far_sent = ffn(far, [over_core(piece) for piece in far], *staged)
    to_left, to_right = after([to_left, to_right], far_kept, cost=WAIT)
    far_got = after([*map(over_core, far_sent)], to_left, to_right)

    passed_right = over_y(narrow(wide(far_kept[:half]) + wide(far_got[0])), 1)
    passed_left = over_y(narrow(wide(far_kept[half:]) + wide(far_got[1])), -1)
    last_right = over_y(narrow(near_sum[3] + wide(passed_right)), 1)
    last_left = over_y(narrow(near_sum[2] + wide(passed_left)), -1)
    own_got = jnp.concatenate([over_core(piece) for piece in own_sent], axis=0)
    from_left = wide(jnp.concatenate([last_right, to_right], axis=0))
    from_right = wide(jnp.concatenate([to_left, last_left], axis=0))
    own_total = wide(own_kept) + wide(own_got)
    returned = exchange(narrow(own_total + from_left + from_right))
    (affinity,) = after([affinity], own_kept)
    weights = 2.5 * affinity / jnp.sum(affinity, axis=1, keepdims=True)
    shares = jnp.sum(matches * weights[:, :, None], axis=1)
    coefficients = picked * jnp.repeat(shares.T, slots, axis=0)
    mixed = jnp.dot(
        coefficients.T,
        wide(returned),
        precision=lax.Precision.HIGHEST,
        preferred_element_type=jnp.float32,
    )
    return narrow(mixed)


def solution(mesh):
    return jax.shard_map(
        shards,
        mesh=mesh,
        in_specs=(
            P(("ep", "tp"), None),
            P(("ep", "tp"), None),
            P(("ep", "tp"), None),
            P("ep", None, "tp"),
            P("ep", None, "tp"),
            P("ep", "tp", None),
        ),
        out_specs=P(("ep", "tp"), None),
        check_vma=False,
    )
```

```python
import functools

import jax
import jax.numpy as jnp
from jax import lax
from jax.experimental import pallas as pl
from jax.experimental.pallas import tpu as pltpu
from jax.sharding import PartitionSpec as P

MIB = 1024 * 1024
WAIT = 256 * MIB
PART = 32
ANYWHERE = pl.BlockSpec(memory_space=pl.ANY)
ONCHIP = pl.BlockSpec(memory_space=pltpu.VMEM)


def after(values, *first, cost=0):
    return pl.pallas_call(
        lambda *refs: None,
        in_specs=[ANYWHERE] * (len(values) + len(first)),
        out_specs=[ANYWHERE] * len(values),
        out_shape=[jax.ShapeDtypeStruct(value.shape, value.dtype) for value in values],
        input_output_aliases={place: place for place in range(len(values))},
        compiler_params=pltpu.CompilerParams(vmem_limit_bytes=MIB),
        cost_estimate=pl.CostEstimate(flops=cost * 64, bytes_accessed=cost, transcendentals=0),
    )(*values, *first)


def taken(value, *first):
    def kernel(*refs):
        refs[-1][...] = refs[0][...]

    return pl.pallas_call(
        kernel,
        in_specs=[ONCHIP] + [ANYWHERE] * len(first),
        out_specs=ONCHIP,
        out_shape=jax.ShapeDtypeStruct(value.shape, value.dtype),
        compiler_params=pltpu.CompilerParams(vmem_limit_bytes=MIB),
    )(value, *first)


def stage_kernel(*refs):
    half = len(refs) // 3
    copies = [
        pltpu.make_async_copy(refs[place], refs[half + place], refs[2 * half + place])
        for place in range(half)
    ]
    for copy in copies:
        copy.start()
    for copy in copies:
        copy.wait()


def stage(*weights):
    return pl.pallas_call(
        stage_kernel,
        in_specs=[pl.BlockSpec(memory_space=pltpu.HBM)] * len(weights),
        out_specs=[ONCHIP] * len(weights),
        out_shape=[pltpu.VMEM(weight.shape, weight.dtype) for weight in weights],
        scratch_shapes=[pltpu.SemaphoreType.DMA] * len(weights),
        compiler_params=pltpu.CompilerParams(vmem_limit_bytes=MIB),
    )(*weights)


def ffn_kernel(own_count, other_count, tiles, *refs):
    own_refs, refs = refs[:own_count], refs[own_count:]
    other_refs, refs = refs[:other_count], refs[other_count:]
    gate_ref, up_ref, down_ref, keep_ref, *send_refs = refs
    half, width = keep_ref.shape
    part = half // len(send_refs)
    rows = jnp.concatenate([ref[...] for ref in (*own_refs, *other_refs)], axis=0)
    gate_value = jnp.dot(rows, gate_ref[0], preferred_element_type=jnp.float32)
    up_value = jnp.dot(rows, up_ref[0], preferred_element_type=jnp.float32)
    hidden = gate_value / (1.0 + jnp.exp(-gate_value)) * up_value
    hidden = hidden.astype(jnp.bfloat16)
    for tile in range(tiles):
        span = slice(tile * (width // tiles), (tile + 1) * (width // tiles))
        out = jnp.dot(hidden, down_ref[0, :, span], preferred_element_type=jnp.float32)
        keep_ref[:, span] = out[:half].astype(jnp.bfloat16)
        for place, send_ref in enumerate(send_refs):
            first = half + place * part
            send_ref[:, span] = out[first : first + part].astype(jnp.bfloat16)


def ffn(own, other, gate_weight, up_weight, down_weight):
    half = sum(piece.shape[0] for piece in own)
    width = own[0].shape[1]
    units = gate_weight.shape[2]
    parts = half // PART
    return pl.pallas_call(
        functools.partial(ffn_kernel, len(own), len(other), 4),
        in_specs=[ONCHIP] * (len(own) + len(other) + 3),
        out_specs=[ONCHIP] * (1 + parts),
        out_shape=[jax.ShapeDtypeStruct((half, width), jnp.bfloat16)]
        + [jax.ShapeDtypeStruct((PART, width), jnp.bfloat16)] * parts,
        compiler_params=pltpu.CompilerParams(vmem_limit_bytes=16 * MIB),
        cost_estimate=pl.CostEstimate(flops=0, bytes_accessed=0, transcendentals=0),
    )(*own, *other, gate_weight, up_weight, down_weight)


def shards(tokens, expert_ids, affinity, gate_weight, up_weight, down_weight):
    ep_count = lax.axis_size("ep")
    tp_count = lax.axis_size("tp")
    experts = ep_count // 2
    tok_count, width = tokens.shape
    top_count = expert_ids.shape[1]
    slots = 2 * max(1, tok_count * top_count // experts)
    count = experts * slots
    half = count // 2
    same_core = [[i for i in range(ep_count) if i % 2 == c] for c in range(2)]

    def over_core(value):
        return lax.ppermute(value, "ep", [(i, i ^ 1) for i in range(ep_count)])

    def over_y(value, shift):
        return lax.ppermute(
            value, "tp", [(i, (i + shift) % tp_count) for i in range(tp_count)]
        )

    def exchange(value):
        return lax.all_to_all(
            value, "ep", split_axis=0, concat_axis=0, axis_index_groups=same_core, tiled=True
        )

    def wide(value):
        return value.astype(jnp.float32)

    def narrow(value):
        return value.astype(jnp.bfloat16)

    labels = jnp.arange(experts, dtype=jnp.int32)
    matches = (expert_ids[:, :, None] == labels[None, None, :]).astype(jnp.float32)
    chosen = jnp.sum(matches, axis=1)
    earlier = jnp.cumsum(chosen, axis=0) - chosen
    slot_values = jnp.arange(slots, dtype=jnp.float32)
    picked = chosen.T[:, None, :] * (earlier.T[:, None, :] == slot_values[None, :, None]).astype(
        jnp.float32
    )
    picked = picked.reshape(count, tok_count)
    outgoing = narrow(
        jnp.dot(picked.astype(jnp.bfloat16), tokens, preferred_element_type=jnp.float32)
    )

    staged = stage(gate_weight, up_weight, down_weight)

    own = exchange(outgoing)
    low, high = own[:half], own[half:]
    others = [over_core(low), over_core(high)]
    near = [over_y(low, 1), over_y(high, -1)]
    own_kept, *own_sent = ffn([low, high], others, *staged)
    near = [*after(near, own_kept), over_y(high, 1), over_y(low, -1)]

    far = [over_y(near[0], 1), over_y(near[1], -1)]
    quarter = half // 2
    traded = [over_core(part) for piece in near for part in (piece[:quarter], piece[quarter:])]
    near_kept, *near_sent = ffn(near, traded, *staged)
    far = after(far, near_kept, cost=WAIT)
    *near_got, far_low = after([*map(over_core, near_sent), far[0]], far[1])
    far = [far_low, far[1]]
    near_sum = [
        wide(near_kept[place * half : (place + 1) * half]) + wide(got)
        for place, got in enumerate(near_got)
    ]

    to_left, to_right = over_y(narrow(near_sum[0]), -1), over_y(narrow(near_sum[1]), 1)
    far_kept, *far_sent = ffn(far, [over_core(piece) for piece in far], *staged)
    to_left, to_right = after([to_left, to_right], far_kept, cost=WAIT)
    far_got = after([*map(over_core, far_sent)], to_left, to_right)

    passed_right = over_y(narrow(wide(far_kept[:half]) + wide(far_got[0])), 1)
    passed_left = over_y(narrow(wide(far_kept[half:]) + wide(far_got[1])), -1)
    last_right = over_y(narrow(near_sum[3] + wide(passed_right)), 1)
    last_left = over_y(narrow(near_sum[2] + wide(passed_left)), -1)
    own_got = jnp.concatenate([over_core(piece) for piece in own_sent], axis=0)
    from_left = wide(jnp.concatenate([last_right, to_right], axis=0))
    from_right = wide(jnp.concatenate([to_left, last_left], axis=0))
    own_total = wide(own_kept) + wide(own_got)
    returned = exchange(narrow(own_total + from_left + from_right))
    affinity = taken(affinity, own_kept)
    weights = 2.5 * affinity / jnp.sum(affinity, axis=1, keepdims=True)
    shares = jnp.sum(matches * weights[:, :, None], axis=1)
    coefficients = picked * jnp.repeat(shares.T, slots, axis=0)
    mixed = jnp.dot(
        coefficients.T,
        wide(returned),
        precision=lax.Precision.HIGHEST,
        preferred_element_type=jnp.float32,
    )
    return narrow(mixed)


def solution(mesh):
    return jax.shard_map(
        shards,
        mesh=mesh,
        in_specs=(
            P(("ep", "tp"), None),
            P(("ep", "tp"), None),
            P(("ep", "tp"), None),
            P("ep", None, "tp"),
            P("ep", None, "tp"),
            P("ep", "tp", None),
        ),
        out_specs=P(("ep", "tp"), None),
        check_vma=False,
    )
```
